32 devices in a mesh: blk: 4 (over z), grp: 8 (over y, x, core).
Axes of the slice: x: 2, y: 2, z: 4, core: 2. Of those that a mesh axis runs over, the one named last changes fastest.
Arguments:
- picture_embeddings_raw: bfloat16 [4096, 1152], P(('blk', 'grp')), may hold values from -6 to 6
- caption_feature_input: bfloat16 [4096, 1152], P(('blk', 'grp')), may hold values from -0.29882812 to 0.29882812
- caption_mapping_weights: bfloat16 [1152, 1152], replicated, may hold values from -0.1875 to 0.1875
- sharpness_array: float32 [1], replicated, may hold values from 10 to 40
- affinity_shift: float32 [1], replicated, may hold values from -4 to -1
Outputs:
- text_grad: bfloat16 [4096, 1152], P(('blk', 'grp'))
- head_grad: float32 [1152, 1152], P('grp', 'blk')
The draws below stay inside these ranges and needn't reach their ends.
All inputs are finite; a program needn't handle non-finite values.
Results may differ from the reference program's by a relative error of at most 0.017.
Values may be sent and summed in bfloat16 or wider, within the bound.
A program may use at most 64 MiB of HBM per device.

```python
import math
import jax
import jax.numpy as jnp
from jax import lax

D = 1152
TOK_DEV = 128
PAIR_TOTAL = 4096
N_GRP = 8


def raised(drawn, key, source, target, shards_of, factor):
    def block_of(dim):
        return (jnp.arange(drawn.shape[dim]) // (drawn.shape[dim] // shards_of)).reshape((-1,) + (1,) * (drawn.ndim - 1 - dim))

    near = jax.random.permutation(key, shards_of)[block_of(target)]
    second = (block_of(target) + shards_of // 2) % shards_of
    return jnp.where((block_of(source) == near) | (block_of(source) == second), factor * drawn, drawn)


def levels(own_key, shape, pieces, least, largest):
    loudness, own = 1.0, jax.random.fold_in(own_key, 6)
    for dim, shards_of in pieces:
        heights = jnp.exp(jax.random.uniform(jax.random.fold_in(own, dim), (shards_of,), jnp.float32, least / len(pieces), largest / len(pieces)))
        loudness = loudness * jnp.repeat(heights, shape[dim] // shards_of).reshape([-1 if axis == dim else 1 for axis in range(len(shape))])
    return loudness


def gaussian(own_key, shape, scale, most, shards=(), kind=jnp.bfloat16):
    level = levels(own_key, shape, shards, -0.22, 0.18) if shards else 1.0
    entries = jax.random.normal(own_key, shape, jnp.float32) * scale * level
    return jnp.minimum(jnp.maximum(entries, -most), most).astype(kind)


def gaussian_with(key, shape, deviation, most, pieces, heavy, kind=jnp.bfloat16):
    values = deviation * jax.random.normal(key, shape, jnp.float32)
    if pieces:
        values = values * levels(key, shape, pieces, -0.22, 0.18)
    return jnp.clip(raised(values, jax.random.fold_in(key, 3), *heavy), -most, most).astype(kind)


def setup_inputs(seed: int = 0) -> dict:
    key_list = jax.random.split(jax.random.key(seed), 6)
    return {
        "picture_embeddings_raw": gaussian(key_list[0], (PAIR_TOTAL, D), 1.0, 6.0, ((0, 32),)),
        "caption_feature_input": gaussian_with(key_list[1], (PAIR_TOTAL, D), 0.05, 0.29882812, ((0, 32),), (0, 1, 32, 2.75)),
        "caption_mapping_weights": gaussian(key_list[2], (D, D), D ** -0.5, 0.1875),
        "sharpness_array": jnp.clip(jnp.exp(jax.random.uniform(key_list[3], (1,), jnp.float32, math.log(10.0), math.log(40.0))), 10.0, 40.0),
        "affinity_shift": jnp.clip(jax.random.uniform(key_list[4], (1,), jnp.float32, -4.0, -1.0), -4.0, -1.0),
    }


def unit_rows(values):
    radius = jnp.sqrt(lax.optimization_barrier(jnp.sum(values * values, axis=1, keepdims=True)) + 1e-06)
    return (values / radius, radius)

def pair_grad(images, texts, labels, sharpness_factor, neighbour_distance):
    pair_scores = sharpness_factor * jnp.dot(images, texts.T, preferred_element_type=jnp.float32) + neighbour_distance
    weights = (jax.nn.sigmoid(pair_scores) - labels).astype(jnp.bfloat16)
    return sharpness_factor * lax.dot_general(weights, images, (((0,), (0,)), ((), ())), preferred_element_type=jnp.float32)

def reference(picture_embeddings_raw, caption_feature_input, caption_mapping_weights, sharpness_array, affinity_shift):
    sharpness_factor = sharpness_array[0]
    neighbour_distance = affinity_shift[0]
    count = PAIR_TOTAL // TOK_DEV
    images = unit_rows(picture_embeddings_raw.astype(jnp.float32))[0].astype(jnp.bfloat16).reshape(count, TOK_DEV, D)
    later = jnp.roll(images, -N_GRP, axis=0)
    texts = caption_feature_input.reshape(count, TOK_DEV, D)
    labels = jnp.eye(TOK_DEV, dtype=jnp.float32)

    def step(total, block):
        local_image_vectors, next_img, feats = block
        projected = jnp.dot(feats, caption_mapping_weights, preferred_element_type=jnp.float32)
        unit, radius = unit_rows(projected)
        text_unit = unit.astype(jnp.bfloat16)
        unit_grad = pair_grad(local_image_vectors, text_unit, labels, sharpness_factor, neighbour_distance) + pair_grad(next_img, text_unit, 0.0, sharpness_factor, neighbour_distance)
        row_grad = ((unit_grad - unit * lax.optimization_barrier(jnp.sum(unit * unit_grad, axis=1, keepdims=True))) / radius).astype(jnp.bfloat16)
        grad_rows = lax.dot_general(row_grad, caption_mapping_weights, (((1,), (1,)), ((), ())), preferred_element_type=jnp.float32).astype(jnp.bfloat16)
        head_term = lax.dot_general(feats, row_grad, (((0,), (0,)), ((), ())), preferred_element_type=jnp.float32).astype(jnp.bfloat16)
        head_term = lax.optimization_barrier(head_term)
        total = total + head_term.astype(jnp.float32)
        return (total, grad_rows)
    head_grad, rows = lax.scan(step, jnp.zeros((D, D), jnp.float32), (images, later, texts))
    return (rows.reshape(PAIR_TOTAL, D), head_grad)
```

```python
import functools

import jax
import jax.numpy as jnp
from jax import lax
from jax.experimental import pallas as pl
from jax.experimental.pallas import tpu as pltpu
from jax.sharding import PartitionSpec as P

MESH = pl.DeviceIdType.MESH
F32 = jnp.float32
BF16 = jnp.bfloat16


def unit_rows(values):
    radius = jnp.sqrt(jnp.sum(values * values, axis=1, keepdims=True) + 1e-06)
    return values / radius, radius


def edges_of(depth):
    tiles = depth // 128
    first = (tiles + 1) // 2
    return [0, first * 128, depth]


def kernel(
    n_blk,
    n_grp,
    sharp_ref,
    shift_ref,
    pic_hbm,
    feat_hbm,
    head_hbm,
    text_ref,
    out_ref,
    pic,
    feat,
    head,
    pic_next,
    feat_send,
    feat_all,
    rows_all,
    total,
    term_send,
    term_recv,
    local_sem,
    pic_sem,
    feat_sem,
    rows_sem,
    pair_sem,
    term_sem,
):
    blk, grp = lax.axis_index("blk"), lax.axis_index("grp")
    count, depth = feat.shape
    own_rows, own_cols = out_ref.shape
    chips = n_grp // 2
    chip, core = grp // 2, lax.rem(grp, 2)
    sibling = grp + 1 - 2 * core
    edges = edges_of(depth)
    chunks = len(edges) - 1

    loads = [
        pltpu.make_async_copy(feat_hbm, feat, local_sem.at[0]),
        pltpu.make_async_copy(head_hbm, head, local_sem.at[1]),
        pltpu.make_async_copy(pic_hbm, pic, local_sem.at[2]),
    ]
    for load in loads:
        load.start()

    barrier = pltpu.get_barrier_semaphore()
    for d in range(1, n_blk):
        pl.semaphore_signal(
            barrier, inc=1, device_id=(lax.rem(blk + d, n_blk), grp), device_id_type=MESH
        )
    for d in range(1, n_grp):
        pl.semaphore_signal(
            barrier, inc=1, device_id=(blk, lax.rem(grp + d, n_grp)), device_id_type=MESH
        )
    pl.semaphore_wait(barrier, n_blk + n_grp - 2)

    def send(source, target, sems, index, device):
        copy = pltpu.make_async_remote_copy(
            src_ref=source,
            dst_ref=target,
            send_sem=sems.at[(0,) + index],
            recv_sem=sems.at[(1,) + index],
            device_id=device,
            device_id_type=MESH,
        )
        return copy

    pic_copy = send(pic_hbm, pic_next, pic_sem, (0,), (lax.rem(blk + n_blk - 1, n_blk), grp))
    pic_copy.start()

    sharp, shift = sharp_ref[0], shift_ref[0]
    loads[0].wait()
    turned = feat[...].T
    if feat_send.shape[1] != own_rows:
        feat_send[...] = jnp.zeros_like(feat_send)
    for i in range(n_grp):
        feat_send[i, :own_rows, :] = turned[i * own_rows : (i + 1) * own_rows, :]
    here = pl.ds(pl.multiple_of(grp * count, count), count)
    feat_copies = []
    for d in range(1, n_grp):
        other = lax.rem(grp + d, n_grp)
        copy = send(
            feat_send.at[other], feat_all.at[:, here], feat_sem, (d - 1,), (blk, other)
        )
        copy.start()
        feat_copies.append(copy)
    feat_all[:, here] = feat_send[grp]

    loads[1].wait()
    projected = jnp.dot(feat[...], head[...], preferred_element_type=F32)
    unit, radius = unit_rows(projected)
    text_unit = unit.astype(BF16)

    def pair_grad(raw, labels):
        images = unit_rows(raw.astype(F32))[0].astype(BF16)
        logits = (
            sharp
            * lax.dot_general(
                text_unit, images, (((1,), (1,)), ((), ())), preferred_element_type=F32
            )
            + shift
        )
        weights = (jax.nn.sigmoid(logits) - labels).astype(BF16)
        return sharp * jnp.dot(weights, images, preferred_element_type=F32)

    row = lax.broadcasted_iota(jnp.int32, (count, count), 0)
    column = lax.broadcasted_iota(jnp.int32, (count, count), 1)
    loads[2].wait()
    unit_grad = pair_grad(pic[...], jnp.where(row == column, 1.0, 0.0).astype(F32))
    pic_copy.wait_recv()
    unit_grad = unit_grad + pair_grad(pic_next[...], 0.0)
    row_grad = (
        (unit_grad - unit * jnp.sum(unit * unit_grad, axis=1, keepdims=True)) / radius
    ).astype(BF16)
    rows_all[here, :] = row_grad

    pending = []
    far = []
    for j in range(chunks):
        part = pl.ds(edges[j], edges[j + 1] - edges[j])
        block = rows_all.at[here, part]
        far.append([])
        for d in range(1, chips):
            other = 2 * lax.rem(chip + d, chips) + core
            copy = send(block, block, rows_sem, (j, d - 1), (blk, other))
            copy.start()
            far[j].append(copy)
            pending.append(copy)
        copy = send(block, block, pair_sem, (j, 0), (blk, sibling))
        copy.start()
        pending.append(copy)

    text_ref[...] = lax.dot_general(
        row_grad, head[...], (((1,), (1,)), ((), ())), preferred_element_type=F32
    ).astype(BF16)

    for copy in feat_copies:
        copy.wait_recv()

    term_copies = []
    done = 0
    for j in range(chunks):
        part = pl.ds(edges[j], edges[j + 1] - edges[j])
        passed = []
        for d in range(1, chips):
            far[j][d - 1].wait_recv()
            source = 2 * lax.rem(chip + chips - d, chips) + core
            block = rows_all.at[pl.ds(pl.multiple_of(source * count, count), count), part]
            copy = send(block, block, pair_sem, (j, d), (blk, sibling))
            copy.start()
            passed.append(copy)
            pending.append(copy)
        own = rows_all.at[here, part]
        send(own, own, pair_sem, (j, 0), (blk, sibling)).wait_recv()
        for copy in passed:
            copy.wait_recv()
        total[:, part] = jnp.dot(feat_all[...], rows_all[:, part], preferred_element_type=F32)
        while done < n_blk and (done + 1) * own_cols <= edges[j + 1]:
            target = done
            piece = total[:own_rows, target * own_cols : (target + 1) * own_cols]

            @pl.when(blk == target)
            def _():
                out_ref[...] = piece

            @pl.when(blk != target)
            def _():
                slot = lax.rem(target - blk + n_blk, n_blk) - 1
                term_send[target, :own_rows, :] = piece.astype(BF16)
                send(
                    term_send.at[target],
                    term_recv.at[slot],
                    term_sem,
                    (slot,),
                    (target, grp),
                ).start()

            done += 1

    result = out_ref[...]
    for d in range(1, n_blk):
        send(
            term_send.at[0], term_recv.at[d - 1], term_sem, (d - 1,), (blk, grp)
        ).wait_recv()
        result = result + term_recv[d - 1, :own_rows, :].astype(F32)
    out_ref[...] = result

    pic_copy.wait_send()
    for copy in feat_copies + pending:
        copy.wait_send()
    for d in range(1, n_blk):
        send(
            term_send.at[0], term_recv.at[d - 1], term_sem, (d - 1,), (blk, grp)
        ).wait_send()


def local(n_blk, n_grp, pictures, features, head, sharp, shift):
    count, depth = pictures.shape
    own_rows, own_cols = depth // n_grp, depth // n_blk
    padded = -(-own_rows // 16) * 16
    chunks = len(edges_of(depth)) - 1
    sems = pltpu.SemaphoreType.DMA
    return pl.pallas_call(
        functools.partial(kernel, n_blk, n_grp),
        out_shape=(
            jax.ShapeDtypeStruct((count, depth), BF16),
            jax.ShapeDtypeStruct((own_rows, own_cols), F32),
        ),
        in_specs=[pl.BlockSpec(memory_space=pltpu.SMEM)] * 2
        + [pl.BlockSpec(memory_space=pl.ANY)] * 3,
        out_specs=(
            pl.BlockSpec(memory_space=pltpu.VMEM),
            pl.BlockSpec(memory_space=pltpu.VMEM),
        ),
        scratch_shapes=[
            pltpu.VMEM((count, depth), BF16),
            pltpu.VMEM((count, depth), BF16),
            pltpu.VMEM((depth, depth), BF16),
            pltpu.VMEM((count, depth), BF16),
            pltpu.VMEM((n_grp, padded, count), BF16),
            pltpu.VMEM((padded, n_grp * count), BF16),
            pltpu.VMEM((n_grp * count, depth), BF16),
            pltpu.VMEM((padded, depth), F32),
            pltpu.VMEM((n_blk, padded, own_cols), BF16),
            pltpu.VMEM((n_blk - 1, padded, own_cols), BF16),
            sems((3,)),
            sems((2, 1)),
            sems((2, n_grp - 1)),
            sems((2, chunks, n_grp // 2 - 1)),
            sems((2, chunks, n_grp // 2)),
            sems((2, n_blk - 1)),
        ],
        compiler_params=pltpu.CompilerParams(
            collective_id=0, has_side_effects=True, vmem_limit_bytes=40 * 1024 * 1024
        ),
        cost_estimate=pl.CostEstimate(
            flops=8 * count * depth * depth,
            bytes_accessed=2 * depth * (depth + 4 * count),
            transcendentals=2 * count * count,
        ),
    )(sharp, shift, pictures, features, head)


def solution(mesh):
    return jax.shard_map(
        functools.partial(local, mesh.shape["blk"], mesh.shape["grp"]),
        mesh=mesh,
        in_specs=(P(("blk", "grp"), None), P(("blk", "grp"), None), P(), P(), P()),
        out_specs=(P(("blk", "grp"), None), P("grp", "blk")),
        check_vma=False,
    )
```

```python
import functools

import jax
import jax.numpy as jnp
from jax import lax
from jax.experimental import pallas as pl
from jax.experimental.pallas import tpu as pltpu
from jax.sharding import PartitionSpec as P

MESH = pl.DeviceIdType.MESH
F32 = jnp.float32
BF16 = jnp.bfloat16


def unit_rows(values):
    radius = jnp.sqrt(jnp.sum(values * values, axis=1, keepdims=True) + 1e-06)
    return values / radius, radius


def plan(depth, n_blk):
    width = depth // n_blk
    order = sorted(range(n_blk), key=lambda i: min(2 * i, 2 * (n_blk - 1 - i) + 1))
    chunks, pieces, low, high = [], [], 0, depth
    for piece in order:
        first = piece * width // 128 * 128
        last = -(-(piece + 1) * width // 128) * 128
        start, stop = max(first, low), min(last, high)
        if start < stop or not chunks:
            chunks.append((start, stop))
            pieces.append([])
            if start == low:
                low = stop
            else:
                high = start
        pieces[-1].append(piece)
    return chunks, pieces


def kernel(
    n_blk,
    n_grp,
    sharp_ref,
    shift_ref,
    pic_hbm,
    feat_hbm,
    head_hbm,
    text_ref,
    out_ref,
    pic,
    feat,
    head,
    pic_next,
    feat_send,
    feat_all,
    rows_all,
    total,
    term_send,
    term_recv,
    local_sem,
    pic_sem,
    feat_sem,
    rows_sem,
    pair_sem,
    term_sem,
):
    blk, grp = lax.axis_index("blk"), lax.axis_index("grp")
    count, depth = feat.shape
    own_rows, own_cols = out_ref.shape
    chips = n_grp // 2
    chip, core = grp // 2, lax.rem(grp, 2)
    sibling = grp + 1 - 2 * core
    chunks, pieces = plan(depth, n_blk)
    square = chips == 4

    loads = [
        pltpu.make_async_copy(feat_hbm, feat, local_sem.at[0]),
        pltpu.make_async_copy(head_hbm, head, local_sem.at[1]),
        pltpu.make_async_copy(pic_hbm, pic, local_sem.at[2]),
    ]
    for load in loads:
        load.start()

    barrier = pltpu.get_barrier_semaphore()
    for d in range(1, n_blk):
        pl.semaphore_signal(
            barrier, inc=1, device_id=(lax.rem(blk + d, n_blk), grp), device_id_type=MESH
        )
    for d in range(1, n_grp):
        pl.semaphore_signal(
            barrier, inc=1, device_id=(blk, lax.rem(grp + d, n_grp)), device_id_type=MESH
        )
    pl.semaphore_wait(barrier, n_blk + n_grp - 2)

    def send(source, target, sems, index, device):
        copy = pltpu.make_async_remote_copy(
            src_ref=source,
            dst_ref=target,
            send_sem=sems.at[(0,) + index],
            recv_sem=sems.at[(1,) + index],
            device_id=device,
            device_id_type=MESH,
        )
        return copy

    pic_copy = send(pic_hbm, pic_next, pic_sem, (0,), (lax.rem(blk + n_blk - 1, n_blk), grp))
    pic_copy.start()

    sharp, shift = sharp_ref[0], shift_ref[0]
    loads[0].wait()
    turned = feat[...].T
    if feat_send.shape[1] != own_rows:
        feat_send[...] = jnp.zeros_like(feat_send)
    for i in range(n_grp):
        feat_send[i, :own_rows, :] = turned[i * own_rows : (i + 1) * own_rows, :]
    here = pl.ds(pl.multiple_of(grp * count, count), count)
    feat_copies = []
    for d in range(1, n_grp):
        other = lax.rem(grp + d, n_grp)
        copy = send(
            feat_send.at[other], feat_all.at[:, here], feat_sem, (d - 1,), (blk, other)
        )
        copy.start()
        feat_copies.append(copy)
    feat_all[:, here] = feat_send[grp]

    loads[1].wait()
    projected = jnp.dot(feat[...], head[...], preferred_element_type=F32)
    unit, radius = unit_rows(projected)
    text_unit = unit.astype(BF16)

    def pair_grad(raw, labels):
        images = unit_rows(raw.astype(F32))[0].astype(BF16)
        logits = (
            sharp
            * lax.dot_general(
                text_unit, images, (((1,), (1,)), ((), ())), preferred_element_type=F32
            )
            + shift
        )
        weights = (jax.nn.sigmoid(logits) - labels).astype(BF16)
        return sharp * jnp.dot(weights, images, preferred_element_type=F32)

    row = lax.broadcasted_iota(jnp.int32, (count, count), 0)
    column = lax.broadcasted_iota(jnp.int32, (count, count), 1)
    loads[2].wait()
    unit_grad = pair_grad(pic[...], jnp.where(row == column, 1.0, 0.0).astype(F32))
    pic_copy.wait_recv()
    unit_grad = unit_grad + pair_grad(pic_next[...], 0.0)
    row_grad = (
        (unit_grad - unit * jnp.sum(unit * unit_grad, axis=1, keepdims=True)) / radius
    ).astype(BF16)
    rows_all[here, :] = row_grad

    pending = []

    def rows_of(other_chip, other_core, part, start=0, size=count):
        first = (2 * other_chip + other_core) * count + start
        return rows_all.at[pl.ds(pl.multiple_of(first, 16), size), part]

    def go(block, sems, index, device):
        copy = send(block, block, sems, index, device)
        copy.start()
        pending.append(copy)
        return copy

    beside = chip + 1 - 2 * lax.rem(chip, 2)
    above = lax.rem(chip + 2, 4)
    across = 3 - chip
    half = count // 2
    parts = [pl.ds(start, stop - start) for start, stop in chunks]
    far = []

    def first_sends(j):
        block = rows_of(chip, core, parts[j])
        if square:
            far.append(
                [
                    go(block, rows_sem, (j, 0), (blk, 2 * beside + core)),
                    go(block, rows_sem, (j, 1), (blk, 2 * above + core)),
                ]
            )
        else:
            far.append(
                [
                    go(block, rows_sem, (j, d - 1), (blk, 2 * lax.rem(chip + d, chips) + core))
                    for d in range(1, chips)
                ]
            )
        go(block, pair_sem, (j, 0), (blk, sibling))

    def relay(j):
        part = parts[j]
        if square:
            far[j][0].wait_recv()
            there = (blk, 2 * above + core)
            far[j].append(go(rows_of(beside, core, part, 0, half), rows_sem, (j, 2), there))
            go(rows_of(beside, core, part), pair_sem, (j, 1), (blk, sibling))
            far[j][1].wait_recv()
            there = (blk, 2 * beside + core)
            far[j].append(go(rows_of(above, core, part, half, half), rows_sem, (j, 3), there))
            go(rows_of(above, core, part), pair_sem, (j, 2), (blk, sibling))

    def finish(j):
        part = parts[j]
        blocks = [rows_of(chip, core, part)]
        if square:
            blocks += [rows_of(beside, core, part), rows_of(above, core, part)]
            for i in range(2):
                far[j][2 + i].wait_recv()
                block = rows_of(across, core, part, i * half, half)
                go(block, pair_sem, (j, 3 + i), (blk, sibling))
                blocks.append(block)
        else:
            for d in range(1, chips):
                far[j][d - 1].wait_recv()
                block = rows_of(lax.rem(chip + chips - d, chips), core, part)
                go(block, pair_sem, (j, d), (blk, sibling))
                blocks.append(block)
        for i, block in enumerate(blocks):
            send(block, block, pair_sem, (j, i), (blk, sibling)).wait_recv()
        total[:, part] = jnp.dot(feat_all[...], rows_all[:, part], preferred_element_type=F32)
        for target in pieces[j]:
            piece = total[:own_rows, target * own_cols : (target + 1) * own_cols]

            @pl.when(blk == target)
            def _():
                out_ref[...] = piece

            @pl.when(blk != target)
            def _():
                slot = lax.rem(target - blk + n_blk, n_blk) - 1
                term_send[target, :own_rows, :] = piece.astype(BF16)
                send(
                    term_send.at[target],
                    term_recv.at[slot],
                    term_sem,
                    (slot,),
                    (target, grp),
                ).start()

    ahead = min(2, len(chunks))
    for j in range(ahead):
        first_sends(j)

    text_ref[...] = lax.dot_general(
        row_grad, head[...], (((1,), (1,)), ((), ())), preferred_element_type=F32
    ).astype(BF16)

    for copy in feat_copies:
        copy.wait_recv()

    for j in range(len(chunks)):
        relay(j)
        if j + ahead < len(chunks):
            first_sends(j + ahead)
        if j:
            finish(j - 1)
    finish(len(chunks) - 1)

    result = out_ref[...]
    for d in range(1, n_blk):
        send(
            term_send.at[0], term_recv.at[d - 1], term_sem, (d - 1,), (blk, grp)
        ).wait_recv()
        result = result + term_recv[d - 1, :own_rows, :].astype(F32)
    out_ref[...] = result

    pic_copy.wait_send()
    for copy in feat_copies + pending:
        copy.wait_send()
    for d in range(1, n_blk):
        send(
            term_send.at[0], term_recv.at[d - 1], term_sem, (d - 1,), (blk, grp)
        ).wait_send()


def local(n_blk, n_grp, pictures, features, head, sharp, shift):
    count, depth = pictures.shape
    own_rows, own_cols = depth // n_grp, depth // n_blk
    padded = -(-own_rows // 16) * 16
    chunks = len(plan(depth, n_blk)[0])
    sems = pltpu.SemaphoreType.DMA
    return pl.pallas_call(
        functools.partial(kernel, n_blk, n_grp),
        out_shape=(
            jax.ShapeDtypeStruct((count, depth), BF16),
            jax.ShapeDtypeStruct((own_rows, own_cols), F32),
        ),
        in_specs=[pl.BlockSpec(memory_space=pltpu.SMEM)] * 2
        + [pl.BlockSpec(memory_space=pltpu.HBM)] * 3,
        out_specs=(
            pl.BlockSpec(memory_space=pltpu.VMEM),
            pl.BlockSpec(memory_space=pltpu.VMEM),
        ),
        scratch_shapes=[
            pltpu.VMEM((count, depth), BF16),
            pltpu.VMEM((count, depth), BF16),
            pltpu.VMEM((depth, depth), BF16),
            pltpu.VMEM((count, depth), BF16),
            pltpu.VMEM((n_grp, padded, count), BF16),
            pltpu.VMEM((padded, n_grp * count), BF16),
            pltpu.VMEM((n_grp * count, depth), BF16),
            pltpu.VMEM((padded, depth), F32),
            pltpu.VMEM((n_blk, padded, own_cols), BF16),
            pltpu.VMEM((n_blk - 1, padded, own_cols), BF16),
            sems((3,)),
            sems((2, 1)),
            sems((2, n_grp - 1)),
            sems((2, chunks, max(4, n_grp // 2 - 1))),
            sems((2, chunks, max(5, n_grp // 2))),
            sems((2, n_blk - 1)),
        ],
        compiler_params=pltpu.CompilerParams(
            collective_id=0, has_side_effects=True, vmem_limit_bytes=60 * 1024 * 1024
        ),
        cost_estimate=pl.CostEstimate(
            flops=8 * count * depth * depth,
            bytes_accessed=2 * depth * (depth + 4 * count),
            transcendentals=2 * count * count,
        ),
    )(sharp, shift, pictures, features, head)


def solution(mesh):
    return jax.shard_map(
        functools.partial(local, mesh.shape["blk"], mesh.shape["grp"]),
        mesh=mesh,
        in_specs=(P(("blk", "grp"), None), P(("blk", "grp"), None), P(), P(), P()),
        out_specs=(P(("blk", "grp"), None), P("grp", "blk")),
        check_vma=False,
    )
```
